32 devices in a mesh: dp: 8 (over z, y), tensor: 4 (over x, core).
Axes of the slice: x: 2, y: 2, z: 4, core: 2. Of those that a mesh axis runs over, the one named last changes fastest.
Arguments:
- layer_input: bfloat16 [2048, 8, 1536], P('tensor', 'dp'), may hold values from -6 to 6
- cotangent: bfloat16 [2048, 8, 1536], P('tensor', 'dp'), may hold values from -6 to 6
- lengths: int32 [8], P('dp'), may hold values from 1024 to 2048, as said below
- owners: int32 [8], replicated, may hold values from 0 to 7, each once
- weight: float32 [1536, 4, 6208], P('dp', 'tensor')
- weight_first: float32 [1536, 4, 6208], P('dp', 'tensor')
- weight_second: float32 [1536, 4, 6208], P('dp', 'tensor'), as said below
- left_basis: float32 [1536, 4, 192], P('dp', 'tensor'), as said below
- right_basis: float32 [8, 4, 97, 64, 64], P('dp', 'tensor'), as said below
- left_stat: float32 [1536, 4, 192], P('dp', 'tensor'), as said below
- right_stat: float32 [8, 4, 97, 64, 64], P('dp', 'tensor'), as said below
- norm_gains: float32 [3200], replicated
- gain_first: float32 [3200], replicated
- gain_second: float32 [3200], replicated, as said below
Outputs:
- layer_output: bfloat16 [2048, 8, 1536], P('tensor', 'dp')
- input_grad: float32 [2048, 8, 1536], P('tensor', 'dp')
- new_weight: float32 [1536, 4, 6208], P('dp', 'tensor')
- new_first: float32 [1536, 4, 6208], P('dp', 'tensor')
- new_second: float32 [1536, 4, 6208], P('dp', 'tensor')
- basis_left: float32 [1536, 4, 192], P('dp', 'tensor')
- basis_right: float32 [8, 4, 97, 64, 64], P('dp', 'tensor')
- stats_left: float32 [1536, 4, 192], P('dp', 'tensor')
- stats_right: float32 [8, 4, 97, 64, 64], P('dp', 'tensor')
- gain_moment: float32 [3200], replicated
- gain_square: float32 [3200], replicated
- new_gains: float32 [3200], replicated
The draws below stay inside these ranges and needn't reach their ends.
Inputs may be any that keep to these rules, and one draw needn't show every extreme that they name: `lengths`: every slot holds 1024 live tokens or more; in every draw some slot is full. `owners`: each number once. `left_basis`: each 192 x 192 block of one row block and tensor index is orthogonal. `right_basis`: each 64 x 64 block is orthogonal. `left_stat`: each 192 x 192 block is symmetric with a dominant positive diagonal. `right_stat`: each 64 x 64 block is symmetric with a dominant positive diagonal. `weight_second`: positive. `gain_second`: positive.
All inputs are finite; a program needn't handle non-finite values.
Results may differ from the reference program's by a relative error of at most 0.012.
The reference program's roundings to bfloat16 on the way count: a program that leaves them out, or rounds other values in their place, can miss the bound.
Values may be sent and summed in bfloat16 or wider, within the bound.
A program may use at most 448 MiB of HBM per device.

```python
import math
import jax
import jax.numpy as jnp
from jax import lax

MODEL_DIM = 1536
QUERY_HEADS = 24
KEY_VALUE_HEADS = 8
HEAD_DIM = 64
FF = 6912
SLOT_POSITIONS = 2048
QUERY_BLOCK = 512
TILE = 64
STEP = 10
BLOCKS = 8
TENSORS = 4
SLOTS = 8
QCOL = 384
KCOL = 128
FCOL = 1728
WCOLS = 6208
WTILES = 97
OWN_ROWS = 192
GAINS = 3200


GRAD_SHARE = (1.0, 1.0, 1.5, 0.27, 0.3, 0.6)


def live_count():
    return SLOTS * SLOT_POSITIONS * 0.75


def column_values(column_ids, per_kind):
    bounds = (QCOL, QCOL + KCOL, QCOL + 2 * KCOL, QCOL + 2 * KCOL + 2 * FCOL, 2 * QCOL + 2 * KCOL + 2 * FCOL)
    result = jnp.full(column_ids.shape, per_kind[5], jnp.float32)
    for position in range(4, -1, -1):
        result = jnp.where(column_ids < bounds[position], per_kind[position], result)
    return result


def grad_columns():
    column_ids = jnp.arange(WCOLS)[None, None, :]
    return column_values(column_ids, GRAD_SHARE) * math.sqrt(live_count())


def cosine_basis(key, lead, size_n):
    rows_n = jnp.arange(size_n, dtype=jnp.float32)[:, None]
    freqs = jnp.arange(size_n, dtype=jnp.float32)[None, :]
    scaling = jnp.where(freqs == 0, math.sqrt(1.0 / size_n), math.sqrt(2.0 / size_n))
    table = jnp.cos(math.pi * (rows_n + 0.5) * freqs / size_n) * scaling
    key_row, key_col = jax.random.split(key)
    row_sign = jnp.where(jax.random.bernoulli(key_row, 0.5, lead + (size_n, 1)), 1.0, -1.0)
    col_sign = jnp.where(jax.random.bernoulli(key_col, 0.5, lead + (1, size_n)), 1.0, -1.0)
    return row_sign * table * col_sign


def dominant(key, lead, size_n, diag_scale):
    key_diag, key_off = jax.random.split(key)
    diagonal = diag_scale * jnp.exp(jax.random.uniform(key_diag, lead + (size_n,), jnp.float32, 0.0, math.log(4.0)))
    spread = jax.random.uniform(key_off, lead + (size_n, size_n), jnp.float32, -1.0, 1.0)
    spread = 0.5 * (spread + jnp.swapaxes(spread, -1, -2))
    identity = jnp.eye(size_n, dtype=jnp.float32)
    return identity * diagonal[..., None] + (1.0 - identity) * spread * (0.95 / max(size_n - 1, 1)) * diag_scale[..., None]


def gain_scales():
    entry_index = jnp.arange(GAINS)
    counted_total = live_count()
    return jnp.where(entry_index < MODEL_DIM, 1.44 * math.sqrt(counted_total), jnp.where(entry_index < 2 * MODEL_DIM, 0.8 * math.sqrt(counted_total), jnp.where(entry_index < 2 * MODEL_DIM + HEAD_DIM, 0.8 * math.sqrt(counted_total * QUERY_HEADS), math.sqrt(counted_total * KEY_VALUE_HEADS))))


def draw_lengths(key, part):
    key = jax.random.fold_in(key, 3)
    key_len, key_pick = jax.random.split(key)
    drawn = jax.random.randint(key_len, (SLOTS,), SLOT_POSITIONS // 2, SLOT_POSITIONS + 1, dtype=jnp.int32)
    full_slot = jax.random.randint(key_pick, (), 0, SLOTS, dtype=jnp.int32)
    return jnp.where(jnp.arange(SLOTS, dtype=jnp.int32) == full_slot, SLOT_POSITIONS, drawn).astype(jnp.int32)


def draw_weight(key, part):
    key = jax.random.fold_in(key, 11)
    column_ids = jnp.arange(WCOLS)[None, None, :]
    in_scale = MODEL_DIM ** (-0.5)
    per_kind = (in_scale, in_scale, in_scale, in_scale, (QUERY_HEADS * HEAD_DIM / 8.0) ** (-0.5), FF ** (-0.5))
    scale_cols = column_values(column_ids, per_kind)
    base = jax.random.normal(key, (MODEL_DIM, TENSORS, WCOLS), jnp.float32)
    return base * scale_cols


def draw_weight_first(key, part):
    key = jax.random.fold_in(key, 13)
    base = jax.random.normal(key, (MODEL_DIM, TENSORS, WCOLS), jnp.float32)
    return base * grad_columns()


def draw_weight_second(key, part):
    key = jax.random.fold_in(key, 17)
    factor = jnp.exp(jax.random.uniform(key, (MODEL_DIM, TENSORS, WCOLS), jnp.float32, math.log(0.5), math.log(8.0)))
    scale_cols = grad_columns()
    return factor * scale_cols * scale_cols


def draw_left_basis(key, part):
    key = jax.random.fold_in(key, 19)
    block_list = cosine_basis(key, (BLOCKS, TENSORS), OWN_ROWS)
    return block_list.transpose(0, 2, 1, 3).reshape(MODEL_DIM, TENSORS, OWN_ROWS)


def draw_right_basis(key, part):
    key = jax.random.fold_in(key, 23)
    return cosine_basis(key, (BLOCKS, TENSORS, WTILES), TILE)


def draw_left_stat(key, part):
    key = jax.random.fold_in(key, 29)
    squares = live_count() * (QCOL * 1.0 + KCOL * 1.0 + KCOL * 2.25 + 2 * FCOL * 0.0729 + QCOL * 0.09 + FCOL * 0.36)
    diag_scale = jnp.full((1, 1, 1), squares, jnp.float32)
    block_list = dominant(key, (BLOCKS, TENSORS), OWN_ROWS, diag_scale)
    return block_list.transpose(0, 2, 1, 3).reshape(MODEL_DIM, TENSORS, OWN_ROWS)


def draw_right_stat(key, part):
    key = jax.random.fold_in(key, 31)
    tile_share = column_values(jnp.arange(WTILES) * TILE, GRAD_SHARE)
    diag_scale = (tile_share * tile_share * OWN_ROWS * live_count()).reshape(1, 1, WTILES, 1)
    return dominant(key, (BLOCKS, TENSORS, WTILES), TILE, diag_scale)


def draw_norm_gains(key, part):
    key = jax.random.fold_in(key, 37)
    entry_index = jnp.arange(GAINS)
    centre = jnp.where(entry_index < 2 * MODEL_DIM, 1.0, 1.4)
    noise = jnp.clip(0.15 * jax.random.normal(key, (GAINS,), jnp.float32), -0.3, 0.3)
    return centre * (1.0 + noise)


def draw_gain_first(key, part):
    key = jax.random.fold_in(key, 41)
    base = jax.random.normal(key, (GAINS,), jnp.float32)
    return base * gain_scales()


def draw_gain_second(key, part):
    key = jax.random.fold_in(key, 43)
    factor = jnp.exp(jax.random.uniform(key, (GAINS,), jnp.float32, math.log(0.5), math.log(8.0)))
    scales = gain_scales()
    return factor * scales * scales


def level_of(own_key, shape, cuts, least, high):
    loudness, own = 1.0, jax.random.fold_in(own_key, 6)
    for axis_at, shards_of in cuts:
        heights = jnp.exp(jax.random.uniform(jax.random.fold_in(own, axis_at), (shards_of,), jnp.float32, least / len(cuts), high / len(cuts)))
        loudness = loudness * jnp.repeat(heights, shape[axis_at] // shards_of).reshape([-1 if axis == axis_at else 1 for axis in range(len(shape))])
    return loudness


def normal_values(rng, dims, scale, most, cuts=(), held_as=jnp.bfloat16):
    values = jax.random.normal(rng, dims, jnp.float32) * scale
    if len(cuts) > 0:
        values = level_of(rng, dims, cuts, -0.22, 0.18) * values
    return jnp.clip(values, min=-most, max=most).astype(held_as)


def setup_inputs(seed: int = 0) -> dict:
    keys = jax.random.split(jax.random.key(seed), 15)
    return {
        "layer_input": normal_values(keys[0], (SLOT_POSITIONS, SLOTS, MODEL_DIM), 1.0, 6.0, ((0, 4), (1, 8))),
        "cotangent": normal_values(keys[1], (SLOT_POSITIONS, SLOTS, MODEL_DIM), 1.0, 6.0, ((0, 4), (1, 8))),
        "lengths": draw_lengths(jax.random.fold_in(keys[14], 71), 0),
        "owners": jax.random.permutation(keys[3], BLOCKS).astype(jnp.int32),
        "weight": draw_weight(jax.random.fold_in(keys[14], 71), 0),
        "weight_first": draw_weight_first(jax.random.fold_in(keys[14], 71), 0),
        "weight_second": draw_weight_second(jax.random.fold_in(keys[14], 71), 0),
        "left_basis": draw_left_basis(jax.random.fold_in(keys[14], 71), 0),
        "right_basis": draw_right_basis(jax.random.fold_in(keys[14], 71), 0),
        "left_stat": draw_left_stat(jax.random.fold_in(keys[14], 71), 0),
        "right_stat": draw_right_stat(jax.random.fold_in(keys[14], 71), 0),
        "norm_gains": draw_norm_gains(jax.random.fold_in(keys[14], 71), 0),
        "gain_first": draw_gain_first(jax.random.fold_in(keys[14], 71), 0),
        "gain_second": draw_gain_second(jax.random.fold_in(keys[14], 71), 0),
    }


NORM_EPS = 1e-06
ROPE_THETA = 1000000.0
MOMENT_DECAY = 0.5
ADAM_EPSILON = 1e-08
RATE_WEIGHT = 0.05
RATE_GAIN = 0.3
DECAY_WEIGHT = 0.01
MASKED_SCORE = -1e+30
PRECISE = lax.Precision.HIGHEST

@jax.custom_vjp
def lowered_rank(v):
    return lax.optimization_barrier(v.astype(jnp.bfloat16)).astype(jnp.float32)

@jax.custom_vjp
def lowered_backward(v):
    return v

def low_keep(v):
    return (lowered_rank(v), None)

def low_pass(kept, grad):
    return (grad,)

def back_keep(v):
    return (v, None)

def back_low(kept, grad):
    return (lowered_rank(grad),)
lowered_rank.defvjp(low_keep, low_pass)
lowered_backward.defvjp(back_keep, back_low)

def matrix_product(form, left, right):
    return jnp.einsum(form, left, right, precision=PRECISE)

def rms_scale(values, gain_vec):
    return values * lax.rsqrt(lax.optimization_barrier(jnp.mean(values * values, axis=-1, keepdims=True)) + NORM_EPS) * gain_vec

def rope_tables(positions_count):
    half_dim = HEAD_DIM // 2
    frequency = ROPE_THETA ** (-(jnp.arange(half_dim, dtype=jnp.float32) * 2.0 / HEAD_DIM))
    angles = jnp.arange(positions_count, dtype=jnp.float32)[:, None] * frequency[None, :]
    return (jnp.cos(angles), jnp.sin(angles))

def rotate(values, cosine, sine):
    half_dim = values.shape[-1] // 2
    table_shape = (cosine.shape[0],) + (1,) * (values.ndim - 2) + (half_dim,)
    cos_rows = cosine.reshape(table_shape)
    sin_rows = sine.reshape(table_shape)
    lower_half = values[..., :half_dim]
    upper_half = values[..., half_dim:]
    return jnp.concatenate([lower_half * cos_rows - upper_half * sin_rows, upper_half * cos_rows + lower_half * sin_rows], axis=-1)

def attend_block(query_block, key_matrix, value_matrix, offset, slot_length):
    scores = lowered_backward(matrix_product('qhgd,khd->hgqk', query_block, key_matrix) * HEAD_DIM ** (-0.5))
    query_pos = offset + jnp.arange(query_block.shape[0], dtype=jnp.int32)
    key_pos = jnp.arange(key_matrix.shape[0], dtype=jnp.int32)
    allowed = (key_pos[None, :] <= query_pos[:, None]) & (key_pos[None, :] < slot_length)
    scores = jnp.where(allowed, scores, MASKED_SCORE)
    row_top = lax.optimization_barrier(jnp.max(scores, axis=-1, keepdims=True))
    exponent = jnp.exp(scores - row_top)
    attn_prob = lowered_rank(exponent / lax.optimization_barrier(jnp.sum(exponent, axis=-1, keepdims=True)))
    return matrix_product('hgqk,khd->qhgd', attn_prob, value_matrix)

def attention_fn(query_matrix, key_matrix, value_matrix, slot_length):
    block_list = SLOT_POSITIONS // QUERY_BLOCK
    query_block_list = query_matrix.reshape(block_list, QUERY_BLOCK, KEY_VALUE_HEADS, QUERY_HEADS // KEY_VALUE_HEADS, HEAD_DIM)
    offsets = jnp.arange(block_list, dtype=jnp.int32) * QUERY_BLOCK

    def one_block(block_items):
        return jax.checkpoint(attend_block)(block_items[0], key_matrix, value_matrix, block_items[1], slot_length)
    outputs = lax.map(one_block, (query_block_list, offsets))
    return outputs.reshape(SLOT_POSITIONS, QUERY_HEADS * HEAD_DIM)

def columns(joined_w, offset, col_count):
    return joined_w[:, :, offset:offset + col_count].reshape(MODEL_DIM, TENSORS * col_count)

def block_forward(joined_w, gain_all, layer_x, slot_length, cosine, sine):
    low_w = lowered_rank(joined_w)
    off_gate = QCOL + 2 * KCOL
    off_out = off_gate + 2 * FCOL
    w_query = columns(low_w, 0, QCOL)
    key_weight = columns(low_w, QCOL, KCOL)
    value_weight = columns(low_w, QCOL + KCOL, KCOL)
    w_gate = columns(low_w, off_gate, FCOL)
    w_up = columns(low_w, off_gate + FCOL, FCOL)
    w_out = columns(low_w, off_out, QCOL)
    w_down = columns(low_w, off_out + QCOL, FCOL)
    gain_in = gain_all[:MODEL_DIM]
    gain_mid = gain_all[MODEL_DIM:2 * MODEL_DIM]
    gain_query = gain_all[2 * MODEL_DIM:2 * MODEL_DIM + HEAD_DIM]
    gain_key = gain_all[2 * MODEL_DIM + HEAD_DIM:]
    normalized_input = lowered_rank(rms_scale(layer_x, gain_in))
    query_matrix = lowered_backward(matrix_product('xe,eg->xg', normalized_input, w_query)).reshape(SLOT_POSITIONS, QUERY_HEADS, HEAD_DIM)
    key_matrix = lowered_backward(matrix_product('xe,eg->xg', normalized_input, key_weight)).reshape(SLOT_POSITIONS, KEY_VALUE_HEADS, HEAD_DIM)
    value_matrix = lowered_rank(lowered_backward(matrix_product('xe,eg->xg', normalized_input, value_weight))).reshape(SLOT_POSITIONS, KEY_VALUE_HEADS, HEAD_DIM)
    query_matrix = lowered_rank(rotate(rms_scale(query_matrix, gain_query), cosine, sine))
    key_matrix = lowered_rank(rotate(rms_scale(key_matrix, gain_key), cosine, sine))
    attended_output = lowered_rank(lowered_backward(attention_fn(query_matrix.reshape(SLOT_POSITIONS, KEY_VALUE_HEADS, QUERY_HEADS // KEY_VALUE_HEADS, HEAD_DIM), key_matrix, value_matrix, slot_length)))
    resid_mid = layer_x + lowered_backward(matrix_product('tc,dc->td', attended_output, w_out))
    normed_mid = lowered_rank(rms_scale(resid_mid, gain_mid))
    gate_val = lowered_backward(matrix_product('xe,eg->xg', normed_mid, w_gate))
    up_val = lowered_backward(matrix_product('xe,eg->xg', normed_mid, w_up))
    hidden = lowered_rank(jax.nn.silu(gate_val) * up_val)
    return resid_mid + lowered_backward(matrix_product('tc,dc->td', hidden, w_down))

def orthonormal(matrix):
    gram_matrix = jnp.einsum('...ik,...il->...kl', matrix, matrix, precision=PRECISE)
    factor = jnp.linalg.cholesky(gram_matrix)
    return lax.linalg.triangular_solve(factor, matrix, left_side=False, lower=True, transpose_a=True)

def precondition(grad_w, weight_w, first_w, second_w, left_w, right_w, left_cov, right_cov):
    shards, own_rows, tensor_parts, cols_all = grad_w.shape
    tile_count = right_w.shape[2]
    tile_width = right_w.shape[3]
    tiled = grad_w.reshape(shards, own_rows, tensor_parts, tile_count, tile_width)
    half_turn = jnp.einsum('sitj,sitbc->sjtbc', left_w, tiled, precision=PRECISE)
    turned = jnp.einsum('sjtbc,stbce->sjtbe', half_turn, right_w, precision=PRECISE).reshape(grad_w.shape)
    first_new = MOMENT_DECAY * first_w + (1.0 - MOMENT_DECAY) * turned
    second_new = MOMENT_DECAY * second_w + (1.0 - MOMENT_DECAY) * turned * turned
    correction = 1.0 - MOMENT_DECAY ** STEP
    direction = first_new / correction / (jnp.sqrt(second_new / correction) + ADAM_EPSILON)
    back_half = jnp.einsum('sitj,sjtbe->sitbe', left_w, direction.reshape(tiled.shape), precision=PRECISE)
    update = jnp.einsum('sitbe,stbce->sitbc', back_half, right_w, precision=PRECISE).reshape(grad_w.shape)
    weight_new = weight_w - RATE_WEIGHT * (update + DECAY_WEIGHT * weight_w)
    left_cov_new = MOMENT_DECAY * left_cov + (1.0 - MOMENT_DECAY) * jnp.einsum('sitbc,sjtbc->sitj', tiled, tiled, precision=PRECISE)
    right_cov_new = MOMENT_DECAY * right_cov + (1.0 - MOMENT_DECAY) * jnp.einsum('sitbc,sitbe->stbce', tiled, tiled, precision=PRECISE)
    left_new = orthonormal(jnp.einsum('sitj,sjtk->stik', left_cov_new, left_w, precision=PRECISE)).transpose(0, 2, 1, 3)
    right_new = orthonormal(jnp.einsum('stbce,stbef->stbcf', right_cov_new, right_w, precision=PRECISE))
    return (weight_new, first_new, second_new, left_new, right_new, left_cov_new, right_cov_new)

def adam_gains(gain_all, gain_grad, first_g, second_g):
    first_new = MOMENT_DECAY * first_g + (1.0 - MOMENT_DECAY) * gain_grad
    second_new = MOMENT_DECAY * second_g + (1.0 - MOMENT_DECAY) * gain_grad * gain_grad
    correction = 1.0 - MOMENT_DECAY ** STEP
    gain_new = gain_all - RATE_GAIN * (first_new / correction) / (jnp.sqrt(second_new / correction) + ADAM_EPSILON)
    return (first_new, second_new, gain_new)

def reference(layer_input, cotangent, lengths, owners, weight, weight_first, weight_second, left_basis, right_basis, left_stat, right_stat, norm_gains, gain_first, gain_second):
    row_blocks = weight.reshape(BLOCKS, OWN_ROWS, TENSORS, WCOLS)
    true_weight = row_blocks[owners].reshape(MODEL_DIM, TENSORS, WCOLS)
    cosine, sine = rope_tables(SLOT_POSITIONS)
    slot_inputs = jnp.moveaxis(layer_input, 1, 0).astype(jnp.float32)
    slot_cots = jnp.moveaxis(cotangent, 1, 0).astype(jnp.float32)

    def one_slot(carry, slot_items):
        layer_x, cot_x, slot_length = slot_items

        def forward(joined_w, gain_all, layer_in):
            return block_forward(joined_w, gain_all, layer_in, slot_length, cosine, sine)
        layer_y, pull_back = jax.vjp(forward, true_weight, norm_gains, layer_x)
        live = (jnp.arange(SLOT_POSITIONS, dtype=jnp.int32) < slot_length).astype(jnp.float32)[:, None]
        grad_w, grad_gain, grad_x = pull_back(cot_x * live)
        return ((carry[0] + grad_w, carry[1] + grad_gain), (layer_y.astype(jnp.bfloat16), grad_x))
    start_carry = (jnp.zeros(true_weight.shape, jnp.float32), jnp.zeros(norm_gains.shape, jnp.float32))
    (weight_grad, gain_grad), (outputs, input_grads) = lax.scan(one_slot, start_carry, (slot_inputs, slot_cots, lengths))
    layer_output = jnp.moveaxis(outputs, 0, 1)
    input_grad = jnp.moveaxis(input_grads, 0, 1)
    grad_blocks = weight_grad.reshape(BLOCKS, OWN_ROWS, TENSORS, WCOLS)
    owner_grad = jnp.zeros_like(grad_blocks).at[owners].set(grad_blocks)
    results = precondition(owner_grad, weight.reshape(owner_grad.shape), weight_first.reshape(owner_grad.shape), weight_second.reshape(owner_grad.shape), left_basis.reshape(BLOCKS, OWN_ROWS, TENSORS, OWN_ROWS), right_basis, left_stat.reshape(BLOCKS, OWN_ROWS, TENSORS, OWN_ROWS), right_stat)
    weight_new, first_new, second_new, left_new, right_new, left_cov_new, right_cov_new = results
    gain_moment, gain_square, new_gains = adam_gains(norm_gains, gain_grad, gain_first, gain_second)
    return (layer_output, input_grad, weight_new.reshape(MODEL_DIM, TENSORS, WCOLS), first_new.reshape(MODEL_DIM, TENSORS, WCOLS), second_new.reshape(MODEL_DIM, TENSORS, WCOLS), left_new.reshape(MODEL_DIM, TENSORS, OWN_ROWS), right_new, left_cov_new.reshape(MODEL_DIM, TENSORS, OWN_ROWS), right_cov_new, gain_moment, gain_square, new_gains)
```

```python
import functools

import jax
import jax.numpy as jnp
from jax import lax
from jax.experimental import pallas as pl
from jax.experimental.pallas import tpu as pltpu
from jax.sharding import PartitionSpec as P

MODEL_DIM = 1536
QUERY_HEADS = 24
KEY_VALUE_HEADS = 8
HEAD_DIM = 64
FF = 6912
STEP = 10

NORM_EPS = 1e-06
ROPE_THETA = 1000000.0
MOMENT_DECAY = 0.5
ADAM_EPSILON = 1e-08
RATE_WEIGHT = 0.05
RATE_GAIN = 0.3
DECAY_WEIGHT = 0.01
MASKED_SCORE = -1e30
PRECISE = lax.Precision.HIGHEST
F32 = jnp.float32
BF16 = jnp.bfloat16
VMEM_LIMIT = 60 * 1024 * 1024
NT = (((1,), (1,)), ((), ()))
TN = (((0,), (0,)), ((), ()))


def params(*kinds):
    return pltpu.CompilerParams(dimension_semantics=kinds, vmem_limit_bytes=VMEM_LIMIT)


def rms_rows(values, gain_vec):
    inverse = lax.rsqrt(jnp.mean(values * values, axis=-1, keepdims=True) + NORM_EPS)
    scaled = values * inverse
    return (scaled * gain_vec, scaled, inverse)


def norm_back(grad_norm, scaled, inverse, gain_vec):
    grad_scaled = grad_norm * gain_vec
    row_inner = jnp.mean(grad_scaled * scaled, axis=-1, keepdims=True)
    return inverse * (grad_scaled - scaled * row_inner)


def rope_tables(positions_count):
    half_dim = HEAD_DIM // 2
    frequency = ROPE_THETA ** (-(jnp.arange(half_dim, dtype=F32) * 2.0 / HEAD_DIM))
    angles = jnp.arange(positions_count, dtype=F32)[:, None] * frequency[None, :]
    return (jnp.cos(angles), jnp.sin(angles))


def lane_tables(positions_count):
    cosine, sine = rope_tables(positions_count)
    return jnp.concatenate([cosine] * 4, axis=1), jnp.concatenate([-sine, sine] * 2, axis=1)


def lanes_like(values):
    return lax.broadcasted_iota(jnp.int32, values.shape, 1)


def both_sums(values):
    low = lanes_like(values) < HEAD_DIM
    first = jnp.sum(jnp.where(low, values, 0.0), axis=1, keepdims=True)
    second = jnp.sum(jnp.where(low, 0.0, values), axis=1, keepdims=True)
    return jnp.where(low, first, second)


def turned(values):
    low = (lanes_like(values) & (HEAD_DIM - 1)) < HEAD_DIM // 2
    return jnp.where(low, pltpu.roll(values, 96, 1), pltpu.roll(values, 32, 1))


def pair_inverse(values):
    return lax.rsqrt(both_sums(values * values) * (1.0 / HEAD_DIM) + NORM_EPS)


def only(head, values):
    low = lanes_like(values) < HEAD_DIM
    zero = jnp.zeros_like(values)
    return jnp.where(low, zero, values) if head % 2 else jnp.where(low, values, zero)


def twice(values):
    low = lanes_like(values) < HEAD_DIM
    other = pltpu.roll(values, HEAD_DIM, 1)
    return jnp.where(low, values, other), jnp.where(low, other, values)


MESH_ID = pl.DeviceIdType.MESH
DMA = pltpu.SemaphoreType.DMA
HBM = pl.BlockSpec(memory_space=pl.ANY)


def one_buffer(shape):
    zeros = (0,) * len(shape)
    return pl.BlockSpec(shape, lambda *_: zeros, pipeline_mode=pl.Buffered(1))


def ring_index(place, count):
    place = lax.rem(place + 2 * count, count)
    odd = lax.div(place, count // 2)
    return 2 * place * (1 - odd) + (2 * (count - 1 - place) + 1) * odd


def ring_place(count):
    me = lax.axis_index("dp")
    odd = lax.rem(me, 2)
    half = lax.div(me, 2)
    return half * (1 - odd) + (count - 1 - half) * odd


def ring_neighbours(count):
    place = ring_place(count)
    return [{"dp": ring_index(place + 1, count)}, {"dp": ring_index(place - 1, count)}]


def tensor_ranks():
    rank = lax.axis_index("tensor")
    core, chip = lax.rem(rank, 2), lax.div(rank, 2)
    return (
        rank,
        2 * chip + 1 - core,
        2 * (1 - chip) + core,
        2 * (1 - chip) + 1 - core,
    )


def greet(peers):
    barrier = pltpu.get_barrier_semaphore()
    for peer in peers:
        pl.semaphore_signal(barrier, inc=1, device_id=peer, device_id_type=MESH_ID)
    pl.semaphore_wait(barrier, len(peers))


def tensor_peers():
    _, pair, across, _ = tensor_ranks()
    return [{"tensor": pair}, {"tensor": across}]


def remote(src, dst, send, recv, peer):
    return pltpu.make_async_remote_copy(
        src_ref=src, dst_ref=dst, send_sem=send, recv_sem=recv, device_id=peer, device_id_type=MESH_ID
    )


def row_parts(rows, pieces):
    units = rows // 16
    forward = (units + 1) // 2
    parts = []
    for way, start, size in ((0, 0, forward), (1, forward, units - forward)):
        cuts = [start + size * i // pieces for i in range(pieces + 1)]
        parts += [(way, 16 * lo, 16 * (hi - lo)) for lo, hi in zip(cuts, cuts[1:]) if hi > lo]
    return parts


class RingGather:
    PIECES = 2

    @classmethod
    def scratch(cls, count, rows):
        return [DMA((2, len(row_parts(rows, cls.PIECES)), count - 1)), DMA((1,))]

    def __init__(self, count, shard, whole, sems, local):
        self.count, self.shard, self.whole, self.sems = count, shard, whole, sems
        self.parts = row_parts(shard.shape[0], self.PIECES)
        self.place = ring_place(count)
        self.peers = ring_neighbours(count)
        self.own = pltpu.make_async_copy(shard, whole.at[lax.axis_index("dp")], local.at[0])

    def out(self, step, index):
        way, start, size = self.parts[index]
        block = ring_index(self.place + (step if way else -step), self.count)
        where = self.whole.at[block, pl.ds(start, size)]
        src = self.shard.at[pl.ds(start, size)] if step == 0 else where
        return remote(
            src, where, self.sems.at[0, index, step], self.sems.at[1, index, step], self.peers[way]
        )

    def into(self, step, index):
        way, start, size = self.parts[index]
        block = ring_index(self.place + (step + 1 if way else -step - 1), self.count)
        where = self.whole.at[block, pl.ds(start, size)]
        return remote(
            where, where, self.sems.at[0, index, step], self.sems.at[1, index, step], self.peers[way]
        )

    def begin(self):
        self.own.start()
        for index in range(len(self.parts)):
            self.out(0, index).start()

    def step(self, step):
        for index in range(len(self.parts)):
            self.into(step, index).wait_recv()
            if step < self.count - 2:
                self.out(step + 1, index).start()

    def finish(self):
        self.own.wait()
        for step in range(self.count - 1):
            for index in range(len(self.parts)):
                self.out(step, index).wait_send()


class RingScatter:
    PIECES = 2

    @classmethod
    def scratch(cls, count, rows, cols, loads=True):
        parts = len(row_parts(rows, cls.PIECES))
        slots = [pltpu.VMEM((count - 1, rows, cols), BF16), DMA((2, parts, count - 1))]
        return slots + ([pltpu.VMEM((2, rows, cols), BF16), DMA((parts, count - 1))] if loads else [])

    def __init__(self, count, take, out, slots, sems, held=None, load_sems=None):
        self.count, self.take, self.out_ref = count, take, out
        self.slots, self.sems, self.held, self.load_sems = slots, sems, held, load_sems
        self.parts = row_parts(slots.shape[1], self.PIECES)
        self.place = ring_place(count)
        self.peers = ring_neighbours(count)

    def local(self, step, index):
        way, start, size = self.parts[index]
        block = ring_index(self.place + (step + 1 if way else -step - 1), self.count)
        return self.take(block, start, size)

    def load(self, step, index):
        _, start, size = self.parts[index]
        return pltpu.make_async_copy(
            self.local(step + 1, index),
            self.held.at[step % 2, pl.ds(start, size)],
            self.load_sems.at[index, step],
        )

    def out(self, step, index):
        way, start, size = self.parts[index]
        rows = pl.ds(start, size)
        return remote(
            self.local(0, index) if step == 0 else self.slots.at[step - 1, rows],
            self.slots.at[step, rows],
            self.sems.at[0, index, step],
            self.sems.at[1, index, step],
            self.peers[way],
        )

    def begin(self):
        for index in range(len(self.parts)):
            self.out(0, index).start()
            if self.held is not None:
                for step in range(min(2, self.count - 1)):
                    self.load(step, index).start()

    def step(self, step):
        for index, (way, start, size) in enumerate(self.parts):
            rows = pl.ds(start, size)
            if self.held is None:
                local = self.local(step + 1, index)[...]
            else:
                self.load(step, index).wait()
                local = self.held[step % 2, rows]
            self.out(step, index).wait_recv()
            total = self.slots[step, rows].astype(F32) + local.astype(F32)
            if step == self.count - 2:
                self.out_ref[rows] = total
            else:
                self.slots[step, rows] = total.astype(BF16)
                self.out(step + 1, index).start()
            if self.held is not None and step + 2 < self.count - 1:
                self.load(step + 2, index).start()

    def finish(self):
        for step in range(self.count - 1):
            for index in range(len(self.parts)):
                self.out(step, index).wait_send()


def rows_of(grads, first=0):
    return lambda block, start, size: grads.at[block, pl.ds(first + start, size)]


CHUNKS = 4


class Exchange:
    @staticmethod
    def scratch(rows, cols):
        return [pltpu.VMEM((rows, cols), BF16)] * 5 + [DMA((8, CHUNKS))]

    def __init__(self, parts, to_send, mine, slot_a, slot_b, slot_x, sems):
        self.parts, self.sems = parts, sems
        self.to_send, self.mine = to_send, mine
        self.slot_a, self.slot_b, self.slot_x = slot_a, slot_b, slot_x
        self.size = mine.shape[0] // CHUNKS
        self.ranks = tensor_ranks()
        self.pair, self.across = tensor_peers()

    def rows(self, k):
        return pl.ds(k * self.size, self.size)

    def load_send(self, k):
        rows = self.rows(k)
        return pltpu.make_async_copy(
            self.parts.at[self.ranks[2], rows], self.to_send.at[rows], self.sems.at[0, k]
        )

    def load_mine(self, k):
        rows = self.rows(k)
        return pltpu.make_async_copy(
            self.parts.at[self.ranks[0], rows], self.mine.at[rows], self.sems.at[1, k]
        )

    def copy_a(self, k):
        rows = self.rows(k)
        return remote(
            self.parts.at[self.ranks[3], rows], self.slot_a.at[rows],
            self.sems.at[2, k], self.sems.at[3, k], self.pair,
        )

    def copy_b(self, k):
        rows = self.rows(k)
        return remote(
            self.parts.at[self.ranks[1], rows], self.slot_b.at[rows],
            self.sems.at[4, k], self.sems.at[5, k], self.pair,
        )

    def copy_x(self, k):
        rows = self.rows(k)
        return remote(
            self.to_send.at[rows], self.slot_x.at[rows],
            self.sems.at[6, k], self.sems.at[7, k], self.across,
        )

    def begin(self):
        for k in range(CHUNKS):
            self.load_send(k).start()
            self.copy_a(k).start()
        for k in range(CHUNKS):
            self.load_mine(k).start()
            self.copy_b(k).start()

    def forward(self, k):
        self.load_send(k).wait()
        self.copy_a(k).wait_recv()
        rows = self.rows(k)
        self.to_send[rows] = (
            self.to_send[rows].astype(F32) + self.slot_a[rows].astype(F32)
        ).astype(BF16)
        self.copy_x(k).start()

    def result(self, k):
        self.load_mine(k).wait()
        self.copy_b(k).wait_recv()
        self.copy_x(k).wait_recv()
        rows = self.rows(k)
        return (
            self.mine[rows].astype(F32) + self.slot_b[rows].astype(F32)
        ) + self.slot_x[rows].astype(F32)

    def finish(self):
        for k in range(CHUNKS):
            self.copy_a(k).wait_send()
            self.copy_b(k).wait_send()
            self.copy_x(k).wait_send()


class Spread:
    @staticmethod
    def scratch():
        return [DMA((7, CHUNKS))]

    def __init__(self, own, whole, sems):
        self.own, self.whole, self.sems = own, whole, sems
        self.size = own.shape[0] // CHUNKS
        self.ranks = tensor_ranks()
        self.pair, self.across = tensor_peers()

    def rows(self, k):
        return pl.ds(k * self.size, self.size)

    def local(self, k):
        rows = self.rows(k)
        return pltpu.make_async_copy(
            self.own.at[rows], self.whole.at[self.ranks[0], rows], self.sems.at[0, k]
        )

    def to_peer(self, k, kind):
        rows = self.rows(k)
        return remote(
            self.own.at[rows], self.whole.at[self.ranks[0], rows],
            self.sems.at[1 + 2 * kind, k], self.sems.at[2 + 2 * kind, k],
            self.across if kind else self.pair,
        )

    def on(self, k):
        rows = self.rows(k)
        where = self.whole.at[self.ranks[2], rows]
        return remote(where, where, self.sems.at[5, k], self.sems.at[6, k], self.pair)

    def send(self, k):
        self.to_peer(k, 1).start()
        self.to_peer(k, 0).start()
        self.local(k).start()

    def forward(self, k):
        self.to_peer(k, 1).wait_recv()
        self.on(k).start()

    def finish(self):
        for k in range(CHUNKS):
            self.local(k).wait()
            self.to_peer(k, 0).wait()
            self.to_peer(k, 1).wait_send()
            self.on(k).wait()


def timed(calls, first, last):
    gap = (last - first) / max(len(calls) - 1, 1)
    return [(first + i * gap, call) for i, call in enumerate(calls)]


def merge(*lists):
    for _, call in sorted(sum(lists, []), key=lambda entry: entry[0]):
        call()


def at_grid(now, ends, *lists):
    plan = {}
    for time, call in sorted(sum(lists, []), key=lambda entry: entry[0]):
        when = next((i for i, end in enumerate(ends) if end >= time), len(ends) - 1)
        plan.setdefault(when, []).append(call)
    for when, calls in plan.items():

        @pl.when(now == when)
        def _(calls=calls):
            for call in calls:
                call()


def comm_params(ident):
    return pltpu.CompilerParams(
        collective_id=ident, has_side_effects=True, vmem_limit_bytes=VMEM_LIMIT
    )


def steps_of(ring, gap, start=0.0):
    gap = gap * 7 / (ring.count - 1)
    return [
        (start + gap * (s + 1), functools.partial(ring.step, s)) for s in range(ring.count - 1)
    ]


def front_kernel(count, a_ref, wa_ref, a_all, wa_all, *scratch):
    greet(tensor_peers() + ring_neighbours(count))
    ring = RingGather(count, wa_ref, wa_all, *scratch[0:2])
    spread = Spread(a_ref, a_all, scratch[2])
    ring.begin()
    for k in range(CHUNKS):
        spread.send(k)
    moves = [functools.partial(spread.forward, k) for k in range(CHUNKS)]
    merge(steps_of(ring, 4.2), timed(moves, 20, 32))
    ring.finish()
    spread.finish()


def front(count, normed, w_attn):
    rows, width = normed.shape
    shape = jax.ShapeDtypeStruct
    return pl.pallas_call(
        functools.partial(front_kernel, count),
        in_specs=[HBM] * 2,
        out_specs=[HBM] * 2,
        out_shape=[shape((4, rows, width), BF16), shape((count,) + w_attn.shape, BF16)],
        scratch_shapes=RingGather.scratch(count, w_attn.shape[0]) + Spread.scratch(),
        compiler_params=comm_params(1),
        name="front",
    )(normed, w_attn)


def rms_of(values):
    return lax.rsqrt(jnp.mean(values * values, axis=-1, keepdims=True) + NORM_EPS)


def middle_kernel(count, part, x_ref, g_ref, wu_ref, wd_ref, h_ref, a_all, wu_all, wd_all, own, *scratch):
    greet(tensor_peers() + ring_neighbours(count))
    exchange = Exchange(part, *scratch[0:6])
    spread = Spread(own, a_all, scratch[6])
    ring_u = RingGather(count, wu_ref, wu_all, *scratch[7:9])
    ring_d = RingGather(count, wd_ref, wd_all, *scratch[9:11])
    exchange.begin()
    ring_u.begin()
    ring_d.begin()

    def land(k):
        rows = exchange.rows(k)
        value = x_ref[rows].astype(F32) + exchange.result(k)
        h_ref[rows] = value
        own[rows] = (value * rms_of(value) * g_ref[...]).astype(BF16)
        spread.send(k)

    def each(call):
        return [functools.partial(call, k) for k in range(CHUNKS)]

    merge(
        timed(each(exchange.forward), 0, 1),
        timed(each(land), 30, 34),
        timed(each(spread.forward), 62, 66),
        steps_of(ring_u, 10.5),
        steps_of(ring_d, 10.5),
    )
    for item in (exchange, spread, ring_u, ring_d):
        item.finish()


def middle(count, part, x, gain, shard_u, shard_d):
    rows, width = x.shape
    shape = jax.ShapeDtypeStruct
    vmem = pl.BlockSpec(memory_space=pltpu.VMEM)
    return pl.pallas_call(
        functools.partial(middle_kernel, count),
        in_specs=[HBM, vmem, vmem, HBM, HBM],
        out_specs=[vmem, HBM, HBM, HBM],
        out_shape=[
            shape((rows, width), F32),
            shape((4, rows, width), BF16),
            shape((count,) + shard_u.shape, BF16),
            shape((count,) + shard_d.shape, BF16),
        ],
        scratch_shapes=[pltpu.VMEM((rows, width), BF16)]
        + Exchange.scratch(rows, width)
        + Spread.scratch()
        + RingGather.scratch(count, shard_u.shape[0])
        + RingGather.scratch(count, shard_d.shape[0]),
        compiler_params=comm_params(2),
        name="middle",
    )(part, x, gain, shard_u, shard_d)


def feed_forward_kernel(a_ref, dy_ref, wg_ref, wu_ref, wd_ref, hid_ref, da_ref, acc):
    cols = wg_ref.shape[1]
    a2, dy = a_ref[...], dy_ref[...]
    for start in range(0, cols, 256):
        part = slice(start, min(start + 256, cols))
        wg, wu = wg_ref[:, part], wu_ref[:, part]
        gate = jnp.dot(a2, wg, preferred_element_type=F32)
        up = jnp.dot(a2, wu, preferred_element_type=F32)
        grad = jnp.dot(dy, wd_ref[:, part], preferred_element_type=F32)
        sig = jax.nn.sigmoid(gate)
        silu = gate * sig
        hid_ref[0, :, part] = (silu * up).astype(BF16)
        d_gate = (grad * up * sig * (1.0 + gate * (1.0 - sig))).astype(BF16)
        d_up = (grad * silu).astype(BF16)
        hid_ref[1, :, part] = d_gate
        hid_ref[2, :, part] = d_up
        back = lax.dot_general(d_gate, wg, NT, preferred_element_type=F32) + lax.dot_general(
            d_up, wu, NT, preferred_element_type=F32
        )
        if start == 0:
            acc[...] = back
        else:
            acc[...] += back
    da_ref[...] = acc[...].astype(BF16)


FF_ROWS = 512


def feed_forward(a2, dy, w_gate, w_up, w_down):
    seq, width = a2.shape
    cols = w_gate.shape[1]
    rows = pl.BlockSpec((FF_ROWS, width), lambda i: (i, 0))
    return pl.pallas_call(
        feed_forward_kernel,
        grid=(seq // FF_ROWS,),
        in_specs=[rows, rows] + [one_buffer((width, cols))] * 3,
        out_specs=[pl.BlockSpec((3, FF_ROWS, cols), lambda i: (0, i, 0)), rows],
        out_shape=[
            jax.ShapeDtypeStruct((3, seq, cols), BF16),
            jax.ShapeDtypeStruct((seq, width), BF16),
        ],
        scratch_shapes=[pltpu.VMEM((FF_ROWS, width), F32)],
        compiler_params=params("arbitrary"),
        cost_estimate=pl.CostEstimate(
            flops=10 * seq * width * cols, bytes_accessed=8 * seq * (width + cols), transcendentals=seq * cols
        ),
        name="feed_forward",
    )(a2, dy, w_gate, w_up, w_down)


M_COLS = 256


def turn_kernel(
    count, own_rows, ff_steps, dyt_ref, a_ref, rhs_ref, hid_ref, w_ref, part, h_ref, dy_ref, g_ref,
    dgu_ref, ffn_ref, d_ref, gain_ref, z_all, sum_ref, own, d_down, *scratch
):
    now = pl.program_id(0)
    cuts = w_ref.shape[0] // M_COLS
    exchange = Exchange(part, *scratch[0:6])
    spread = Spread(own, z_all, scratch[6])

    def take(block, start, size):
        return d_down.at[pl.ds(pl.multiple_of(block * own_rows + start, 16), size)]

    ring = RingScatter(count, take, sum_ref, *scratch[7:9])

    @pl.when(now == 0)
    def _():
        greet(tensor_peers() + ring_neighbours(count))
        exchange.begin()
        gain_ref[...] = jnp.zeros_like(gain_ref)

    @pl.when(now < cuts)
    def _():
        at = pl.multiple_of(now * M_COLS, M_COLS)
        d_down[pl.ds(at, M_COLS)] = lax.dot_general(
            dyt_ref[...], rhs_ref[0], TN, preferred_element_type=F32
        ).astype(BF16)

    @pl.when((now >= cuts) & (now < 3 * cuts))
    def _():
        dgu_ref[0] = lax.dot_general(
            a_ref[...], rhs_ref[0], TN, preferred_element_type=F32
        ).astype(BF16)

    @pl.when(now >= 3 * cuts)
    def _():
        ffn_ref[...] = lax.dot_general(
            hid_ref[0], w_ref[...], NT, preferred_element_type=F32
        ).astype(BF16)

    def land(k):
        rows = exchange.rows(k)
        grad = exchange.result(k)
        value = h_ref[rows]
        inverse = rms_of(value)
        scaled = value * inverse
        gain_ref[...] += jnp.sum(grad * scaled, axis=0, keepdims=True)
        back = dy_ref[rows].astype(F32) + norm_back(grad, scaled, inverse, g_ref[...])
        d_ref[rows] = back
        own[rows] = back.astype(BF16)
        spread.send(k)

    def each(call):
        return [functools.partial(call, k) for k in range(CHUNKS)]

    total = 3 * cuts + ff_steps
    ends = [2.7 * (i + 1) for i in range(total)]
    at_grid(
        now,
        ends,
        timed(each(exchange.forward), 3, 3),
        timed(each(land), 33, 36),
        timed(each(spread.forward), 66, 69),
        [(ends[cuts - 1], ring.begin)],
        steps_of(ring, 7.0, ends[cuts - 1]),
    )

    @pl.when(now == total - 1)
    def _():
        for item in (exchange, spread, ring):
            item.finish()


def turn(count, part, h, dy, gain, dy_all, a_all, hidden3, w_down):
    rows, width = h.shape
    _, seq, cols = hidden3.shape
    own = width // count
    cuts = width // M_COLS
    ff_rows = 256
    ff_steps = seq // ff_rows
    shape = jax.ShapeDtypeStruct

    def within(i, low, high):
        return jnp.minimum(jnp.maximum(i - low, 0), high)

    def gu_block(i):
        at = within(i, cuts, 2 * cuts - 1)
        return lax.div(at, cuts), lax.rem(at, cuts)

    def ff_block(i):
        return within(i, 3 * cuts, ff_steps - 1)

    return pl.pallas_call(
        functools.partial(turn_kernel, count, own, ff_steps),
        grid=(3 * cuts + ff_steps,),
        in_specs=[
            pl.BlockSpec((seq, M_COLS), lambda i: (0, within(i, 0, cuts - 1))),
            pl.BlockSpec((seq, M_COLS), lambda i: (0, gu_block(i)[1])),
            pl.BlockSpec(
                (1, seq, cols),
                lambda i: (jnp.minimum(lax.div(i, cuts), 2), 0, 0),
                pipeline_mode=pl.Buffered(1),
            ),
            pl.BlockSpec((1, ff_rows, cols), lambda i: (0, ff_block(i), 0)),
            one_buffer(w_down.shape),
            HBM,
            one_buffer(h.shape),
            one_buffer(h.shape),
            one_buffer(gain.shape),
        ],
        out_specs=[
            pl.BlockSpec((1, M_COLS, cols), lambda i: gu_block(i) + (0,)),
            pl.BlockSpec((ff_rows, width), lambda i: (ff_block(i), 0)),
            one_buffer(h.shape),
            one_buffer(gain.shape),
            HBM,
            one_buffer((own, cols)),
        ],
        out_shape=[
            shape((2, width, cols), BF16),
            shape((seq, width), BF16),
            shape((rows, width), F32),
            shape((1, width), F32),
            shape((4, rows, width), BF16),
            shape((own, cols), F32),
        ],
        scratch_shapes=[pltpu.VMEM((rows, width), BF16), pltpu.VMEM((width, cols), BF16)]
        + Exchange.scratch(rows, width)
        + Spread.scratch()
        + RingScatter.scratch(count, own, cols, loads=False),
        compiler_params=comm_params(3),
        name="turn",
    )(dy_all, a_all, hidden3, hidden3, w_down, part, h, dy, gain)


def last_kernel(
    count, first, part, x_ref, d_ref, g_ref, grads_u, grads_a, out_ref, gain_ref, sum_u, sum_a, *scratch
):
    greet(tensor_peers() + ring_neighbours(count))
    exchange = Exchange(part, *scratch[0:6])
    ring_u = RingScatter(count, rows_of(grads_u.at[1], first), sum_u, *scratch[6:10])
    ring_a = RingScatter(count, rows_of(grads_a), sum_a, *scratch[10:14])
    exchange.begin()
    ring_u.begin()
    ring_a.begin()
    gain_ref[...] = jnp.zeros_like(gain_ref)

    def land(k):
        rows = exchange.rows(k)
        grad = exchange.result(k)
        value = x_ref[rows].astype(F32)
        inverse = rms_of(value)
        scaled = value * inverse
        gain_ref[...] += jnp.sum(grad * scaled, axis=0, keepdims=True)
        out_ref[rows] = d_ref[rows] + norm_back(grad, scaled, inverse, g_ref[...])

    def each(call):
        return [functools.partial(call, k) for k in range(CHUNKS)]

    merge(
        timed(each(exchange.forward), 0, 1),
        timed(each(land), 33, 36),
        steps_of(ring_u, 7.6),
        steps_of(ring_a, 7.6),
    )
    for item in (exchange, ring_u, ring_a):
        item.finish()


def last(count, part, x, d, gain, grads_u, first, grads_a):
    rows, width = x.shape
    _, _, own, cols = grads_u.shape
    shape = jax.ShapeDtypeStruct
    vmem = pl.BlockSpec(memory_space=pltpu.VMEM)
    return pl.pallas_call(
        functools.partial(last_kernel, count, first),
        in_specs=[HBM, vmem, vmem, vmem, HBM, HBM],
        out_specs=[vmem, vmem, vmem, vmem],
        out_shape=[
            shape((rows, width), F32),
            shape((1, width), F32),
            shape((own - first, cols), F32),
            shape(grads_a.shape[1:], F32),
        ],
        scratch_shapes=Exchange.scratch(rows, width)
        + RingScatter.scratch(count, own - first, cols)
        + RingScatter.scratch(*grads_a.shape),
        compiler_params=comm_params(4),
        name="last",
    )(part, x, d, gain, grads_u, grads_a)


GROUPS = 2
GROUP = QUERY_HEADS // KEY_VALUE_HEADS
HEADS = GROUPS * GROUP
Q_COLS = HEADS * HEAD_DIM
QK_COLS = Q_COLS + GROUPS * HEAD_DIM
QKV_COLS = QK_COLS + GROUPS * HEAD_DIM
Q_ROWS = 256
K_STEP = 512


def pair_of(head):
    return slice(128 * (head // 2), 128 * (head // 2) + 128)


def attend_kernel(
    count, blocks, a_ref, w_ref, gq_ref, gk_ref, cos_ref, sin_ref, bias_ref, dy_ref, wg_ref, wd_ref,
    part_ref, q_ref, k_ref, v_ref, raw_ref, o_ref, lse_ref, dy_all, wg_all, wd_all,
    k_scr, v_scr, s_scr, m_scr, l_scr, acc_scr, *scratch
):
    rows = a_ref.shape[0]
    seq = k_scr.shape[1]
    step = min(K_STEP, seq)
    tall = GROUP * rows
    block = pl.program_id(0)
    ends = [5.0 + 2.1 * (1 + (i * rows) // step) for i in range(blocks)]
    ends = [sum(ends[: i + 1]) for i in range(len(ends))]
    ring_g = RingGather(count, wg_ref, wg_all, *scratch[0:2])
    ring_d = RingGather(count, wd_ref, wd_all, *scratch[2:4])
    spread = Spread(dy_ref, dy_all, scratch[4])

    @pl.when(block == 0)
    def _():
        k_scr[...] = jnp.zeros_like(k_scr)
        v_scr[...] = jnp.zeros_like(v_scr)
        greet(tensor_peers() + ring_neighbours(count))
        ring_g.begin()
        ring_d.begin()
        for k in range(CHUNKS):
            spread.send(k)

    raw = jnp.dot(a_ref[...], w_ref[:, :QKV_COLS], preferred_element_type=F32)
    raw_ref[...] = raw[:, :QK_COLS]
    cosine, sine = cos_ref[...], sin_ref[...]

    def roped(values, gain):
        normed = values * pair_inverse(values) * gain
        return normed * cosine + turned(normed) * sine

    for head in range(0, HEADS, 2):
        q_ref[:, pair_of(head)] = roped(raw[:, pair_of(head)], gq_ref[...]).astype(
            BF16
        ) * HEAD_DIM ** (-0.5)
    key = roped(raw[:, Q_COLS:QK_COLS], gk_ref[...])
    value = raw[:, QK_COLS:]
    k_ref[...] = key.astype(BF16)
    v_ref[...] = value.astype(BF16)
    here = pl.ds(pl.multiple_of(block * rows, rows), rows)
    for group, (one_key, one_value) in enumerate(zip(twice(key), twice(value))):
        k_scr[group, here] = one_key.astype(BF16)
        v_scr[group, here] = one_value.astype(BF16)

    last_block = lax.div(block * rows, step)
    at_last = pl.multiple_of(last_block * step, step)
    for group in range(GROUPS):
        heads = range(group * GROUP, group * GROUP + GROUP)
        query = jnp.concatenate([only(head, q_ref[:, pair_of(head)]) for head in heads], axis=0)
        m_scr[...] = jnp.full_like(m_scr, MASKED_SCORE)
        l_scr[...] = jnp.zeros_like(l_scr)
        acc_scr[group] = jnp.zeros_like(acc_scr[group])

        def scores(at, group=group, query=query):
            keys = k_scr[group, pl.ds(at, step), :]
            return lax.dot_general(query, keys, NT, preferred_element_type=F32) + bias_ref[
                :, pl.ds(at, step)
            ]

        def keep(at, found):
            s_scr[:, pl.ds(at, step)] = found
            top = found[:, :128]
            for part in range(1, step // 128):
                top = jnp.maximum(top, found[:, part * 128 : (part + 1) * 128])
            m_scr[...] = jnp.maximum(m_scr[...], top)

        @pl.loop(0, last_block)
        def _(index, scores=scores, keep=keep):
            at = pl.multiple_of(index * step, step)
            keep(at, scores(at))

        found = scores(at_last)
        row_pos = block * rows + (lax.broadcasted_iota(jnp.int32, (tall, step), 0) & (rows - 1))
        key_pos = at_last + lax.broadcasted_iota(jnp.int32, (tall, step), 1)
        keep(at_last, jnp.where(key_pos <= row_pos, found, MASKED_SCORE))
        top = jnp.max(m_scr[...], axis=1, keepdims=True)

        @pl.loop(0, last_block + 1)
        def _(index, group=group, top=top):
            at = pl.multiple_of(index * step, step)
            prob = jnp.exp(s_scr[:, pl.ds(at, step)] - top)
            total = prob[:, :128]
            for part in range(1, step // 128):
                total = total + prob[:, part * 128 : (part + 1) * 128]
            l_scr[...] += total
            acc_scr[group] += jnp.dot(
                prob.astype(BF16), v_scr[group, pl.ds(at, step), :], preferred_element_type=F32
            )

        total = jnp.sum(l_scr[...], axis=1, keepdims=True)
        acc_scr[group] = acc_scr[group] / total
        lse = jnp.broadcast_to(top + jnp.log(total), (tall, 128)).T[0:1, :]
        for i, head in enumerate(heads):
            lse_ref[head : head + 1, :] = lse[:, i * rows : (i + 1) * rows]

    def head_out(head):
        at = (head % GROUP) * rows
        return acc_scr[head // GROUP, at : at + rows, :]

    for head in range(0, HEADS, 2):
        first, second = head_out(head), head_out(head + 1)
        o_ref[:, pair_of(head)] = jnp.where(lanes_like(first) < HEAD_DIM, first, second).astype(BF16)
    part_ref[...] = lax.dot_general(
        o_ref[...], w_ref[:, QKV_COLS:], NT, preferred_element_type=F32
    ).astype(BF16)

    at_grid(
        block,
        ends,
        steps_of(ring_g, 12.0),
        steps_of(ring_d, 12.0),
        timed([functools.partial(spread.forward, k) for k in range(CHUNKS)], 45, 48),
    )

    @pl.when(block == len(ends) - 1)
    def _():
        for item in (ring_g, ring_d, spread):
            item.finish()


def attend(count, a_all, w_attn, gain_q, gain_k, cosine, sine, bias, dy, shard_g, shard_d):
    seq, width = a_all.shape
    blocks = seq // Q_ROWS
    tall = GROUP * Q_ROWS
    shape = jax.ShapeDtypeStruct

    def rows(cols):
        return pl.BlockSpec((Q_ROWS, cols), lambda i: (i, 0))

    return pl.pallas_call(
        functools.partial(attend_kernel, count, blocks),
        grid=(blocks,),
        in_specs=[
            rows(width), one_buffer(w_attn.shape), one_buffer((1, 128)), one_buffer((1, 128)),
            rows(128), rows(128), one_buffer((1, seq)), HBM, HBM, HBM,
        ],
        out_specs=[
            rows(width), rows(Q_COLS), rows(128), rows(128), rows(QK_COLS), rows(Q_COLS),
            pl.BlockSpec((8, Q_ROWS), lambda i: (0, i)), HBM, HBM, HBM,
        ],
        out_shape=[
            shape((seq, width), BF16),
            shape((seq, Q_COLS), BF16),
            shape((seq, 128), BF16),
            shape((seq, 128), BF16),
            shape((seq, QK_COLS), F32),
            shape((seq, Q_COLS), BF16),
            shape((8, seq), F32),
            shape((4,) + dy.shape, BF16),
            shape((count,) + shard_g.shape, BF16),
            shape((count,) + shard_d.shape, BF16),
        ],
        scratch_shapes=[
            pltpu.VMEM((GROUPS, seq, 128), BF16),
            pltpu.VMEM((GROUPS, seq, 128), BF16),
            pltpu.VMEM((tall, seq), F32),
            pltpu.VMEM((tall, 128), F32),
            pltpu.VMEM((tall, 128), F32),
            pltpu.VMEM((GROUPS, tall, 128), F32),
        ]
        + RingGather.scratch(count, shard_g.shape[0])
        + RingGather.scratch(count, shard_d.shape[0])
        + Spread.scratch(),
        compiler_params=comm_params(5),
        name="attend",
    )(a_all, w_attn, gain_q, gain_k, cosine, sine, bias, dy, shard_g, shard_d)


B_ROWS = 512


def causal_pair(at, blocks):
    key_block, start, cum = 0, 0, 0
    for i in range(blocks - 1):
        cum += blocks - i
        past = (at >= cum).astype(jnp.int32)
        key_block = key_block + past
        start = start + past * (blocks - i)
    return key_block, at - start + key_block


def attend_back_kernel(
    count, blocks, q_ref, k_ref, v_ref, raw_ref, o_ref, lse_ref, dz_ref, a_ref, w_ref, gq_ref, gk_ref,
    cos_ref, sin_ref, bias_ref, pick_ref, grads, ffn_part, h_ref,
    part_ref, dw_ref, dgq_ref, dgk_ref, sum_g, sum_u, y_ref,
    do_scr, delta_scr, dq_scr, dk_scr, dv_scr, kd_scr, vd_scr, dwa_scr, dwo_scr, *scratch
):
    rows = k_ref.shape[0]
    now = pl.program_id(0)
    key_block, query_block = causal_pair(now, blocks)
    ring_g = RingScatter(
        count, lambda b, start, size: grads.at[0, b, pl.ds(start, size)], sum_g, *scratch[0:4]
    )
    ring_u = RingScatter(
        count, lambda b, start, size: grads.at[1, b, pl.ds(start, size)], sum_u, *scratch[4:8]
    )
    exchange = Exchange(ffn_part, *scratch[8:14])

    @pl.when(now == 0)
    def _():
        greet(tensor_peers() + ring_neighbours(count))
        exchange.begin()
        ring_g.begin()
        ring_u.begin()
        dq_scr[...] = jnp.zeros_like(dq_scr)
        dgq_ref[...] = jnp.zeros_like(dgq_ref)
        dgk_ref[...] = jnp.zeros_like(dgk_ref)
        dwa_scr[...] = jnp.zeros_like(dwa_scr)
        dwo_scr[...] = jnp.zeros_like(dwo_scr)

    at = pl.multiple_of(query_block * rows, rows)

    @pl.when(key_block == 0)
    def _():
        grad = jnp.dot(dz_ref[...], w_ref[:, QKV_COLS:], preferred_element_type=F32).astype(BF16)
        do_scr[pl.ds(at, rows), :] = grad
        delta_scr[:, pl.ds(at, rows)] = lax.dot_general(
            pick_ref[...], grad.astype(F32) * o_ref[...].astype(F32), NT,
            preferred_element_type=F32, precision=PRECISE,
        )
        dwo_scr[...] += lax.dot_general(dz_ref[...], o_ref[...], TN, preferred_element_type=F32)

    @pl.when(query_block == key_block)
    def _():
        for source, target in ((k_ref, kd_scr), (v_ref, vd_scr)):
            for group, one in enumerate(twice(source[...].astype(F32))):
                target[group] = one.astype(BF16)
        dk_scr[...] = jnp.zeros_like(dk_scr)
        dv_scr[...] = jnp.zeros_like(dv_scr)

    bias = bias_ref[...]

    def one(head, diagonal):
        group = head // GROUP
        query = only(head, q_ref[:, pair_of(head)])
        grad = only(head, do_scr[pl.ds(at, rows), pair_of(head)])
        score = lax.dot_general(kd_scr[group], query, NT, preferred_element_type=F32) + bias
        if diagonal:
            key_pos = lax.broadcasted_iota(jnp.int32, (rows, rows), 0)
            row_pos = lax.broadcasted_iota(jnp.int32, (rows, rows), 1)
            score = jnp.where(key_pos <= row_pos, score, MASKED_SCORE)
        prob = jnp.exp(score - lse_ref[head : head + 1, pl.ds(at, rows)])
        dv_scr[group] += jnp.dot(prob.astype(BF16), grad, preferred_element_type=F32)
        grad_prob = lax.dot_general(vd_scr[group], grad, NT, preferred_element_type=F32)
        grad_score = (prob * (grad_prob - delta_scr[head : head + 1, pl.ds(at, rows)])).astype(BF16)
        dk_scr[group] += jnp.dot(grad_score, query, preferred_element_type=F32)
        dq_scr[pl.ds(at, rows), pair_of(head)] += lax.dot_general(
            grad_score, only(head, kd_scr[group]), TN, preferred_element_type=F32
        )

    @pl.when(query_block == key_block)
    def _():
        for head in range(HEADS):
            one(head, True)

    @pl.when(query_block != key_block)
    def _():
        for head in range(HEADS):
            one(head, False)

    @pl.when(query_block == blocks - 1)
    def _():
        cosine, sine = cos_ref[...], sin_ref[...]

        def back(grad, raw, gain_ref, out_ref):
            grad = grad * cosine - turned(grad) * sine
            inverse = pair_inverse(raw)
            scaled = raw * inverse
            out_ref[...] += jnp.sum(grad * scaled, axis=0, keepdims=True)
            grad = grad * gain_ref[...]
            inner = both_sums(grad * scaled) * (1.0 / HEAD_DIM)
            return (inverse * (grad - scaled * inner)).astype(BF16)

        def joined(halves):
            total = [half + pltpu.roll(half, HEAD_DIM, 1) for half in (halves[0], halves[1])]
            return jnp.where(lanes_like(total[0]) < HEAD_DIM, total[0], total[1])

        mine = pl.ds(pl.multiple_of(key_block * rows, rows), rows)
        grads_qkv = [
            back(
                dq_scr[mine, pair_of(head)] * HEAD_DIM ** (-0.5),
                raw_ref[:, pair_of(head)], gq_ref, dgq_ref,
            )
            for head in range(0, HEADS, 2)
        ]
        grads_qkv.append(back(joined(dk_scr), raw_ref[:, Q_COLS:], gk_ref, dgk_ref))
        grads_qkv.append(joined(dv_scr).astype(BF16))
        grad_qkv = jnp.concatenate(grads_qkv, axis=1)
        part_ref[...] = lax.dot_general(
            grad_qkv, w_ref[:, :QKV_COLS], NT, preferred_element_type=F32
        ).astype(BF16)
        dwa_scr[...] += lax.dot_general(a_ref[...], grad_qkv, TN, preferred_element_type=F32)

    def land(k):
        lines = exchange.rows(k)
        y_ref[lines] = (h_ref[lines] + exchange.result(k)).astype(BF16)

    def each(call):
        return [functools.partial(call, k) for k in range(CHUNKS)]

    costs = []
    for i in range(blocks):
        for j in range(i, blocks):
            costs.append(5.4 + (3.5 if i == 0 else 0.0) + (5.0 if j == blocks - 1 else 0.0))
    ends = [sum(costs[: i + 1]) for i in range(len(costs))]
    at_grid(
        now,
        ends,
        timed(each(exchange.forward), 3, 3),
        timed(each(land), 40, 44),
        steps_of(ring_g, 12.0),
        steps_of(ring_u, 12.0),
    )

    @pl.when(now == len(ends) - 1)
    def _():
        dw_ref[:, :QKV_COLS] = dwa_scr[...].astype(BF16)
        dw_ref[:, QKV_COLS:] = dwo_scr[...].astype(BF16)
        for item in (ring_g, ring_u, exchange):
            item.finish()


def attend_back(
    count, query, key, value, raw, attn, lse, dz_all, a_all, w_attn, gain_q, gain_k, cosine, sine,
    bias_col, grads, up_rows, ffn_part, h
):
    seq, width = a_all.shape
    blocks = seq // B_ROWS
    _, _, own, cols = grads.shape
    shape = jax.ShapeDtypeStruct
    pick = (jnp.arange(8)[:, None] == jnp.arange(Q_COLS)[None, :] // HEAD_DIM).astype(F32)

    def by_key(wide):
        return pl.BlockSpec((B_ROWS, wide), lambda i: (causal_pair(i, blocks)[0], 0))

    def by_query(wide):
        return pl.BlockSpec((B_ROWS, wide), lambda i: (causal_pair(i, blocks)[1], 0))

    def at_first(wide):
        return pl.BlockSpec((B_ROWS, wide), lambda i: (jnp.minimum(i, blocks - 1), 0))

    return pl.pallas_call(
        functools.partial(attend_back_kernel, count, blocks),
        grid=(blocks * (blocks + 1) // 2,),
        in_specs=[
            by_query(Q_COLS), by_key(128), by_key(128), by_key(QK_COLS), at_first(Q_COLS),
            one_buffer((8, seq)), at_first(width), by_key(width), one_buffer(w_attn.shape),
            one_buffer((1, 128)), one_buffer((1, 128)), by_key(128), by_key(128), by_key(1),
            one_buffer((8, Q_COLS)), HBM, HBM, one_buffer(h.shape),
        ],
        out_specs=[
            by_key(width), one_buffer(w_attn.shape), one_buffer((1, 128)), one_buffer((1, 128)),
            one_buffer((own, cols)), one_buffer((up_rows, cols)), one_buffer(h.shape),
        ],
        out_shape=[
            shape((seq, width), BF16),
            shape(w_attn.shape, BF16),
            shape((1, 128), F32),
            shape((1, 128), F32),
            shape((own, cols), F32),
            shape((up_rows, cols), F32),
            shape(h.shape, BF16),
        ],
        scratch_shapes=[
            pltpu.VMEM((seq, Q_COLS), BF16),
            pltpu.VMEM((8, seq), F32),
            pltpu.VMEM((seq, Q_COLS), F32),
            pltpu.VMEM((GROUPS, B_ROWS, 128), F32),
            pltpu.VMEM((GROUPS, B_ROWS, 128), F32),
            pltpu.VMEM((GROUPS, B_ROWS, 128), BF16),
            pltpu.VMEM((GROUPS, B_ROWS, 128), BF16),
            pltpu.VMEM((width, QKV_COLS), F32),
            pltpu.VMEM((width, Q_COLS), F32),
        ]
        + RingScatter.scratch(count, own, cols)
        + RingScatter.scratch(count, up_rows, cols)
        + Exchange.scratch(*h.shape),
        compiler_params=comm_params(6),
        name="attend_back",
    )(
        query, key, value, raw, attn, lse, dz_all, a_all, w_attn, gain_q, gain_k, cosine, sine,
        bias_col, pick, grads, ffn_part, h,
    )


PRE_COLS = 512


def precondition_kernel(
    total_cols, p_ref, w_ref, f_ref, s_ref, l_ref, lt_ref, r_ref, ls_ref, lf_ref,
    wo_ref, fo_ref, so_ref, rso_ref, lso_ref, at_ref,
):
    rows, width = p_ref.shape
    step = pl.program_id(0)
    valid = (
        step * width + lax.broadcasted_iota(jnp.int32, (rows, width), 1) < total_cols
    )
    grad = jnp.where(valid, p_ref[...], 0.0)
    low = grad.astype(BF16)
    half = jnp.dot(lt_ref[...], low, preferred_element_type=F32).astype(BF16)
    pairs = width // 128
    turned = jnp.concatenate(
        [
            jnp.dot(half[:, i * 128 : (i + 1) * 128], r_ref[i], preferred_element_type=F32)
            for i in range(pairs)
        ],
        axis=1,
    )
    first = MOMENT_DECAY * f_ref[...] + (1.0 - MOMENT_DECAY) * turned
    second = MOMENT_DECAY * s_ref[...] + (1.0 - MOMENT_DECAY) * turned * turned
    fo_ref[...] = first
    so_ref[...] = second
    correction = 1.0 - MOMENT_DECAY**STEP
    direction = first / correction / (jnp.sqrt(second / correction) + ADAM_EPSILON)
    direction = jnp.where(valid, direction, 0.0).astype(BF16)
    back = jnp.dot(l_ref[...], direction, preferred_element_type=F32).astype(BF16)
    update = jnp.concatenate(
        [
            lax.dot_general(
                back[:, i * 128 : (i + 1) * 128], r_ref[i], NT, preferred_element_type=F32
            )
            for i in range(pairs)
        ],
        axis=1,
    )
    weight = w_ref[...]
    wo_ref[...] = weight - RATE_WEIGHT * (update + DECAY_WEIGHT * weight)
    for i in range(pairs):
        tile = low[:, i * 128 : (i + 1) * 128]
        cov = lax.dot_general(tile, tile, TN, preferred_element_type=F32)
        for j in range(2):
            rso_ref[2 * i + j] = cov[j * 64 : (j + 1) * 64, j * 64 : (j + 1) * 64]

    @pl.when(step == 0)
    def _():
        lso_ref[...] = MOMENT_DECAY * ls_ref[...]

    lso_ref[...] += (1.0 - MOMENT_DECAY) * lax.dot_general(
        low, low, NT, preferred_element_type=F32
    )

    @pl.when(step == pl.num_programs(0) - 1)
    def _():
        at_ref[...] = lax.dot_general(
            lf_ref[...], lso_ref[...], NT, preferred_element_type=F32, precision=PRECISE
        )


def precondition(grad, weight, first, second, left, pairs, tiles, left_stat):
    rows, cols = grad.shape
    per = PRE_COLS // 64
    flat = pl.BlockSpec((rows, PRE_COLS), lambda i: (0, i))
    deep = pl.BlockSpec((rows, None, PRE_COLS), lambda i: (0, 0, i))
    square = pl.BlockSpec((rows, rows), lambda i: (0, 0))
    right = pl.BlockSpec((per, 64, 64), lambda i: (i, 0, 0))
    left_t = left.T
    return pl.pallas_call(
        functools.partial(precondition_kernel, cols),
        grid=(pl.cdiv(cols, PRE_COLS),),
        in_specs=[
            flat, deep, deep, deep, square, square,
            pl.BlockSpec((per // 2, 128, 128), lambda i: (i, 0, 0)),
            square, square,
        ],
        out_specs=[deep, deep, deep, right, square, square],
        out_shape=[
            jax.ShapeDtypeStruct((rows, 1, cols), F32),
            jax.ShapeDtypeStruct((rows, 1, cols), F32),
            jax.ShapeDtypeStruct((rows, 1, cols), F32),
            jax.ShapeDtypeStruct((tiles, 64, 64), F32),
            jax.ShapeDtypeStruct((rows, rows), F32),
            jax.ShapeDtypeStruct((rows, rows), F32),
        ],
        compiler_params=params("arbitrary"),
        cost_estimate=pl.CostEstimate(
            flops=rows * cols * 2 * 1500, bytes_accessed=rows * cols * 28, transcendentals=rows * cols
        ),
        name="precondition",
    )(grad, weight, first, second, left.astype(BF16), left_t.astype(BF16), pairs, left_stat, left_t)


def right_basis_kernel(cov_ref, old_ref, r_ref, stat_ref, q_ref, norm_ref):
    size = r_ref.shape[0]
    lanes = r_ref.shape[2]
    unroll = 8
    pair = 2

    def start(step, s):
        at = step * pair
        rows = []
        for j in range(pair):
            stat = MOMENT_DECAY * old_ref[at + j] + (1.0 - MOMENT_DECAY) * cov_ref[at + j]
            stat_ref[at + j] = stat
            rows.append(stat)
        sums = [row[0:1] * r_ref[0] for row in rows]
        for k in range(1, size):
            right = r_ref[k]
            sums = [total + row[k : k + 1] * right for total, row in zip(sums, rows)]
        for j in range(pair):
            q_ref[at + j] = sums[j]
            s = s + sums[j] * sums[j][0:1]
        return s

    s = lax.fori_loop(0, size // pair, start, jnp.zeros((size, lanes), F32))
    for k in range(size):
        low = (k // 8) * 8
        nxt = min(((k + 1) // 8) * 8, size - 8)
        squared = s[k - low : k - low + 1]
        norm_ref[k : k + 1] = lax.rsqrt(squared)
        if k == size - 1:
            break
        ids = low + lax.broadcasted_iota(jnp.int32, s.shape, 0)
        coef = jnp.where(ids > k, s / squared, 0.0)

        def update(i, s_next, k=k, low=low, nxt=nxt, coef=coef):
            row = q_ref[i, low:size, :]
            new = row - row[k - low : k - low + 1] * coef
            q_ref[i, low:size, :] = new
            new = new[nxt - low :]
            return s_next + new * new[k + 1 - nxt : k + 2 - nxt]

        s = lax.fori_loop(
            0, size, update, jnp.zeros((size - nxt, s.shape[1]), F32), unroll=unroll
        )
    norms = norm_ref[...]

    def finish(i, carry):
        q_ref[i] = q_ref[i] * norms
        return carry

    lax.fori_loop(0, size, finish, 0, unroll=unroll)


def right_orthonormal(cov, old, right):
    size, _, count = right.shape
    shape = jax.ShapeDtypeStruct(right.shape, F32)
    return pl.pallas_call(
        right_basis_kernel,
        out_shape=[shape, shape],
        scratch_shapes=[pltpu.VMEM((size, count), F32)],
        compiler_params=params(),
        cost_estimate=pl.CostEstimate(
            flops=4 * size**3 * count * 16, bytes_accessed=20 * size * size * 128, transcendentals=0
        ),
        name="right_orthonormal",
    )(cov, old, right)


def left_basis_kernel(panel, a_ref, q_ref):
    rows, width = a_ref.shape
    q_ref[...] = a_ref[...]
    for start in range(0, rows, panel):
        ids = lax.broadcasted_iota(jnp.int32, (panel, 1), 0)

        def step(k, carry, start=start, ids=ids):
            line = q_ref[pl.ds(start + k, 1), :]
            block = q_ref[start : start + panel, :]
            squared = jnp.sum(line * line, axis=1, keepdims=True)
            inner = jnp.sum(block * line, axis=1, keepdims=True)
            coef = jnp.where(ids > k, inner / squared, 0.0)
            q_ref[start : start + panel, :] = block - coef * line
            return carry

        lax.fori_loop(0, panel, step, 0)
        block = q_ref[start : start + panel, :]
        block = block * lax.rsqrt(jnp.sum(block * block, axis=1, keepdims=True))
        q_ref[start : start + panel, :] = block
        if start + panel < rows:
            rest = q_ref[start + panel :, :]
            inner = lax.dot_general(rest, block, NT, preferred_element_type=F32, precision=PRECISE)
            q_ref[start + panel :, :] = rest - jnp.dot(
                inner, block, preferred_element_type=F32, precision=PRECISE
            )


def left_orthonormal(matrix_t):
    rows = matrix_t.shape[0]
    panel = 64 if rows % 64 == 0 else rows
    return pl.pallas_call(
        functools.partial(left_basis_kernel, panel),
        out_shape=jax.ShapeDtypeStruct(matrix_t.shape, F32),
        compiler_params=params(),
        cost_estimate=pl.CostEstimate(
            flops=rows**3 * 200, bytes_accessed=8 * rows * rows, transcendentals=0
        ),
        name="left_orthonormal",
    )(matrix_t)


def sum_everywhere(vector):
    for axis in ("tensor", "dp"):
        count = lax.axis_size(axis)
        bit = 1
        while bit < count:
            vector = vector + lax.ppermute(vector, axis, [(i, i ^ bit) for i in range(count)])
            bit *= 2
    return vector


def mul(left, right, dims=(((1,), (0,)), ((), ())), out=F32):
    return lax.dot_general(left, right, dims, preferred_element_type=F32).astype(out)


def body(
    layer_input, cotangent, lengths, owners, weight, weight_first, weight_second,
    left_basis, right_basis, left_stat, right_stat, norm_gains, gain_first, gain_second,
):
    tensor_total = lax.axis_size("tensor")
    count = lax.axis_size("dp")
    rows_here, slots_here, model_width = layer_input.shape
    assert tensor_total == 4 and slots_here == 1
    seq_all = rows_here * tensor_total
    own_rows, _, cols_all = weight.shape
    query_cols = QUERY_HEADS * HEAD_DIM // tensor_total
    kv_cols = KEY_VALUE_HEADS * HEAD_DIM // tensor_total
    ff_cols = FF // tensor_total
    off_gate = query_cols + 2 * kv_cols
    off_out = off_gate + 2 * ff_cols
    off_down = off_out + query_cols

    ids = jnp.arange(count, dtype=jnp.int32)
    holds = jnp.sum(jnp.where(owners[None, :] == ids[:, None], ids[None, :], 0), axis=1)
    true_column = (holds[:, None] * own_rows + jnp.arange(own_rows, dtype=jnp.int32)[None, :]).reshape(-1)
    move = (jnp.arange(model_width, dtype=jnp.int32)[:, None] == true_column[None, :]).astype(BF16)

    def held_gain(vector):
        return jnp.take(vector.reshape(count, own_rows), holds, axis=0).reshape(1, model_width)

    def true_gain(vector):
        return jnp.take(vector.reshape(count, own_rows), owners, axis=0).reshape(-1)

    weight2 = weight.reshape(own_rows, cols_all)
    low_w = weight2.astype(BF16)
    shard_attn = jnp.concatenate([low_w[:, :off_gate], low_w[:, off_out:off_down]], axis=1)
    shard_gate = low_w[:, off_gate : off_gate + ff_cols]
    shard_up = low_w[:, off_gate + ff_cols : off_out]
    shard_down = low_w[:, off_down:]

    gain_in = held_gain(norm_gains[:MODEL_DIM])
    gain_mid = held_gain(norm_gains[MODEL_DIM : 2 * MODEL_DIM])
    gain_query = norm_gains[2 * MODEL_DIM : 2 * MODEL_DIM + HEAD_DIM]
    gain_key = norm_gains[2 * MODEL_DIM + HEAD_DIM :]
    cosine, sine = lane_tables(seq_all)
    rank = lax.axis_index("tensor")
    positions = rank * rows_here + jnp.arange(rows_here, dtype=jnp.int32)
    live = (positions < lengths[0]).astype(BF16)[:, None]
    x_low = mul(layer_input.reshape(rows_here, model_width), move, out=BF16)
    grad_low = mul(cotangent.reshape(rows_here, model_width) * live, move, out=BF16)
    normed_in = rms_rows(x_low.astype(F32), gain_in)[0].astype(BF16)
    low_in, w_attn = front(count, normed_in, shard_attn)
    low_in = low_in.reshape(seq_all, model_width)
    w_attn = w_attn.reshape(model_width, off_gate + query_cols)
    half_rows = 16 * (own_rows // 32)
    gain_query = jnp.tile(gain_query, 2)[None, :]
    gain_key = jnp.tile(gain_key, 2)[None, :]
    bias = jnp.where(jnp.arange(seq_all, dtype=jnp.int32) < lengths[0], 0.0, MASKED_SCORE).astype(F32)
    attn_part, query, key, value, raw, attn, lse, grad_out_all, w_gate, w_down_a = attend(
        count, low_in, w_attn, gain_query, gain_key, cosine, sine, bias[None, :],
        grad_low, shard_gate, shard_down[:half_rows],
    )
    grad_out_all = grad_out_all.reshape(seq_all, model_width)
    w_gate = w_gate.reshape(model_width, ff_cols)

    ranked = (tensor_total, rows_here, model_width)
    blocked = (count, own_rows)
    attn_part = attn_part.reshape(ranked)
    resid_mid, low_mid, w_up, w_down_b = middle(
        count, attn_part, x_low, gain_mid, shard_up, shard_down[half_rows:]
    )
    low_mid = low_mid.reshape(seq_all, model_width)
    w_up = w_up.reshape(model_width, ff_cols)
    w_down = jnp.concatenate([w_down_a, w_down_b], axis=1).reshape(model_width, ff_cols)

    hidden3, grad_mid_part = feed_forward(low_mid, grad_out_all, w_gate, w_up, w_down)
    d_gu, ffn_part, grad_resid, gain_mid_grad, grad_resid_all, sum_down = turn(
        count, grad_mid_part.reshape(ranked), resid_mid, grad_low, gain_mid,
        grad_out_all, low_mid, hidden3, w_down,
    )
    ffn_part = ffn_part.reshape(ranked)
    d_gu = d_gu.reshape((2,) + blocked + (ff_cols,))

    grad_in_part, d_attn, gain_query_grad, gain_key_grad, sum_gate, sum_up_a, out_held = attend_back(
        count, query, key, value, raw, attn, lse, grad_resid_all.reshape(seq_all, model_width), low_in,
        w_attn, gain_query, gain_key, cosine, sine, bias[:, None], d_gu, half_rows, ffn_part, resid_mid,
    )
    layer_output = mul(out_held, move, NT, BF16)
    d_attn = d_attn.reshape(blocked + (off_gate + query_cols,))
    grad_in_part = grad_in_part.reshape(ranked)
    gain_query_grad = jnp.sum(gain_query_grad.reshape(2, HEAD_DIM), axis=0)
    gain_key_grad = jnp.sum(gain_key_grad.reshape(2, HEAD_DIM), axis=0)
    grad_held, gain_in_grad, sum_up_b, sum_attn = last(
        count, grad_in_part, x_low, grad_resid, gain_in, d_gu, half_rows, d_attn
    )
    sum_up = jnp.concatenate([sum_up_a, sum_up_b], axis=0)
    grad_top = grad_held.astype(BF16)
    grad_rest = (grad_held - grad_top.astype(F32)).astype(BF16)
    input_grad = mul(grad_top, move, NT) + mul(grad_rest, move, NT)

    gain_grad = sum_everywhere(
        jnp.concatenate(
            [true_gain(gain_in_grad), true_gain(gain_mid_grad), gain_query_grad, gain_key_grad]
        )
    )
    moment_one = MOMENT_DECAY * gain_first + (1.0 - MOMENT_DECAY) * gain_grad
    moment_two = MOMENT_DECAY * gain_second + (1.0 - MOMENT_DECAY) * gain_grad * gain_grad
    correction = 1.0 - MOMENT_DECAY**STEP
    gains_new = norm_gains - RATE_GAIN * (moment_one / correction) / (
        jnp.sqrt(moment_two / correction) + ADAM_EPSILON
    )

    grad_own = jnp.concatenate(
        [sum_attn[:, :off_gate], sum_gate, sum_up, sum_attn[:, off_gate:], sum_down], axis=1
    )
    tiles = cols_all // 64
    right = right_basis.reshape(tiles, 64, 64)
    even = jnp.pad(right, ((0, tiles % 2), (0, 0), (0, 0))).astype(BF16).reshape(-1, 2, 64, 64)
    pairs = jnp.concatenate(
        [
            jnp.pad(even[:, 0], ((0, 0), (0, 0), (0, 64))),
            jnp.pad(even[:, 1], ((0, 0), (0, 0), (64, 0))),
        ],
        axis=1,
    )
    weight_new, first_new, second_new, right_cov, left_stat_new, left_a_t = precondition(
        grad_own,
        weight,
        weight_first,
        weight_second,
        left_basis.reshape(own_rows, own_rows),
        pairs,
        tiles,
        left_stat.reshape(own_rows, own_rows),
    )
    left_new = left_orthonormal(left_a_t).T
    right_stat_new, right_new = right_orthonormal(
        right_cov.transpose(1, 2, 0),
        right_stat.reshape(tiles, 64, 64).transpose(1, 2, 0),
        right.transpose(1, 2, 0),
    )
    right_stat_new = right_stat_new.transpose(2, 0, 1)
    right_new = right_new.transpose(2, 0, 1)
    return (
        layer_output.reshape(layer_input.shape),
        input_grad.reshape(layer_input.shape),
        weight_new.reshape(weight.shape),
        first_new.reshape(weight.shape),
        second_new.reshape(weight.shape),
        left_new.reshape(left_basis.shape),
        right_new.reshape(right_basis.shape),
        left_stat_new.reshape(left_stat.shape),
        right_stat_new.reshape(right_stat.shape),
        moment_one,
        moment_two,
        gains_new,
    )


def solution(mesh):
    whole, flat = P(), P("dp", "tensor", None)
    rows, tiles = P("tensor", "dp", None), P("dp", "tensor", None, None, None)
    in_specs = (
        rows, rows, P("dp"), whole, flat, flat, flat, flat, tiles, flat, tiles, whole, whole, whole,
    )
    out_specs = (rows, rows, flat, flat, flat, flat, tiles, flat, tiles, whole, whole, whole)
    return jax.shard_map(body, mesh=mesh, in_specs=in_specs, out_specs=out_specs, check_vma=False)
```
